32 devices in a mesh: sec: 2 (over x), az: 16 (over z, y, core).
Axes of the slice: x: 2, y: 2, z: 4, core: 2. Of those that a mesh axis runs over, the one named last changes fastest.
Arguments:
- axial: float32 [2, 4, 128, 1024], P('sec', None, 'az'), may hold values from -6 to 6
- azimuthal: float32 [2, 4, 128, 1024], P('sec', None, 'az'), may hold values from -6 to 6
- radial: float32 [2, 4, 128, 1024], P('sec', None, 'az'), may hold values from -6 to 6
- drag_blocks: int32 [2, 128, 16], P('sec', 'az'), may hold values 0 or 1
- rotation: int32 [1], replicated, may hold values from 1 to 15
- row_pairs: int32 [8], replicated, may hold values from 0 to 7, each once
Outputs:
- axial_out: float32 [2, 4, 128, 1024], P('sec', None, 'az')
- azimuthal_out: float32 [2, 4, 128, 1024], P('sec', None, 'az')
- radial_out: float32 [2, 4, 128, 1024], P('sec', None, 'az')
The draws below stay inside these ranges and needn't reach their ends.
Inputs may be any that keep to these rules, and one draw needn't show every extreme that they name: rotation is a whole number of azimuthal blocks. row_pairs holds each of 0 to 7 once.
All inputs are finite; a program needn't handle non-finite values. No bound on the sum of `drag_blocks` on one device may be relied on, other than what follows from the above.
Results may differ from the reference program's by a relative error of at most 0.0001.
Values sent between devices are 32-bit elements; how exact they have to be, the bound alone decides.
A program may use at most 64 MiB of HBM per device.

```python
import jax
import jax.numpy as jnp

ROWS_DEV = 8
NR = 1024
LAYERS = 4
STEPS = 2
ITERS = 3
SECTIONS = 2
NA = 128
RBLOCKS = 16
N_AZ = 16


def touch_ends(array, rng, least, top_value):
    longest = array.shape.index(max(array.shape))
    spots = []
    for shift in (0, 1):
        where = [jax.random.randint(jax.random.fold_in(rng, axis), (), 0, length) for axis, length in enumerate(array.shape)]
        where[longest] = (where[longest] + shift) % array.shape[longest]
        spots.append(tuple(where))
    return array.at[spots[0]].set(least).at[spots[1]].set(top_value)


def block_levels(own_key, dims, cuts, smallest, top_value):
    level = 1.0
    for axis_at, shards_of in cuts:
        heights = jax.random.uniform(jax.random.fold_in(jax.random.fold_in(own_key, 6), axis_at), (shards_of,), jnp.float32, smallest / len(cuts), top_value / len(cuts))
        level = level * jnp.repeat(jnp.exp(heights), dims[axis_at] // shards_of).reshape((-1,) + (1,) * (len(dims) - 1 - axis_at))
    return level


def scatter_about(stream_key, shape, deviation, reach, cuts=(), held_as=jnp.bfloat16):
    values = deviation * jax.random.normal(stream_key, shape, jnp.float32)
    if cuts:
        values = values * block_levels(stream_key, shape, cuts, -0.22, 0.18)
    return jnp.clip(values, -reach, reach).astype(held_as)


def setup_inputs(seed: int = 0) -> dict:
    arg_keys = jax.random.split(jax.random.key(seed), 7)
    return {
        "axial": scatter_about(arg_keys[0], (SECTIONS, LAYERS, NA, NR), 1.0, 6.0, ((0, 2), (2, 16)), jnp.float32),
        "azimuthal": scatter_about(arg_keys[1], (SECTIONS, LAYERS, NA, NR), 1.0, 6.0, ((0, 2), (2, 16)), jnp.float32),
        "radial": scatter_about(arg_keys[2], (SECTIONS, LAYERS, NA, NR), 1.0, 6.0, ((0, 2), (2, 16)), jnp.float32),
        "drag_blocks": touch_ends((jax.random.randint(arg_keys[3], (SECTIONS, NA, RBLOCKS), 0, 3) < 1).astype(jnp.int32), jax.random.fold_in(arg_keys[3], 1), 0, 1),
        "rotation": jax.random.randint(arg_keys[4], (1,), 1, N_AZ).astype(jnp.int32),
        "row_pairs": jax.random.permutation(arg_keys[5], ROWS_DEV).astype(jnp.int32),
    }


courant = 0.5
viscosity = 0.1
diagonal_add = 0.05
drag_rate = 2.0
block_cells = 64


def neighbours(field):
    padded = jnp.pad(field, [(0, 0)] * (field.ndim - 1) + [(1, 1)])
    beside = jnp.roll(field, 1, field.ndim - 2) + jnp.roll(field, -1, field.ndim - 2)
    return beside + padded[..., 2:] + padded[..., :-2]


def operate(field, diag_coef):
    return diag_coef * field - neighbours(field)


def layer_sums(values):
    return jnp.sum(values, axis=(1, 2), keepdims=True)


def solve(source, diag_coef):
    solution = jnp.zeros_like(source)
    residual = source
    direction = source
    norm_now = layer_sums(residual * residual)
    for iteration in range(ITERS):
        applied = operate(direction, diag_coef)
        step_size = norm_now / layer_sums(direction * applied)
        solution = solution + step_size * direction
        residual = residual - step_size * applied
        norm_next = layer_sums(residual * residual)
        direction = residual + (norm_next / norm_now) * direction
        norm_now = norm_next
    return solution


def advance(fields, upstream_plane, drag_section):
    upstream = jnp.concatenate([upstream_plane[:, None], fields[:, :-1]], axis=1)
    predicted = fields - courant * (fields - upstream) + viscosity * (neighbours(fields) - 4.0 * fields)
    azimuth_vel = predicted[1]
    radial_vel = predicted[2]
    radial_prev = jnp.pad(radial_vel, ((0, 0), (0, 0), (1, 0)))[..., :-1]
    divergence = (azimuth_vel - jnp.roll(azimuth_vel, 1, 1)) + (radial_vel - radial_prev)
    drag_map = jnp.repeat(drag_section.astype(jnp.float32), block_cells, axis=1)
    diag_coef = 4.0 + diagonal_add + drag_rate * drag_map
    pressure = solve(divergence, diag_coef)
    next_azimuth = jnp.roll(pressure, -1, 1)
    next_radial = jnp.pad(pressure, ((0, 0), (0, 0), (0, 1)))[..., 1:]
    return jnp.stack([predicted[0], azimuth_vel - (next_azimuth - pressure), radial_vel - (next_radial - pressure)])


def reference(axial, azimuthal, radial, drag_blocks, rotation, row_pairs):
    precursor = jnp.stack([axial[0], azimuthal[0], radial[0]])
    sleeve = jnp.stack([axial[1], azimuthal[1], radial[1]])
    for time_step in range(STEPS):
        outlet = precursor[:, -1]
        turn_blocks = (rotation[0] * (time_step + 1)) % N_AZ
        blocks = outlet.reshape(3, N_AZ, ROWS_DEV, NR)
        blocks = jnp.roll(blocks, turn_blocks, axis=1)
        inflow = jnp.take(blocks, row_pairs.astype(jnp.int32), axis=2).reshape(3, NA, NR)
        precursor = advance(precursor, outlet, drag_blocks[0])
        sleeve = advance(sleeve, inflow, drag_blocks[1])
    return (jnp.stack([precursor[0], sleeve[0]]), jnp.stack([precursor[1], sleeve[1]]), jnp.stack([precursor[2], sleeve[2]]))
```

```python
import functools

import jax
import jax.numpy as jnp
from jax import lax
from jax.experimental import pallas as pl
from jax.experimental.pallas import tpu as pltpu
from jax.sharding import PartitionSpec as P

STEPS = 2

courant = 0.5
viscosity = 0.1
diagonal_add = 0.05
drag_rate = 2.0
block_cells = 64
centre = 4.0 + diagonal_add + 0.5 * drag_rate
MESH = pl.DeviceIdType.MESH


def radial_sum(x):
    cells = x.shape[1]
    lane = lax.broadcasted_iota(jnp.int32, x.shape, 1)
    before = jnp.where(lane == 0, 0.0, pltpu.roll(x, 1, 1))
    after = jnp.where(lane == cells - 1, 0.0, pltpu.roll(x, cells - 1, 1))
    return before + after


def step_kernel(
    n, pairs, ax, az, ra, drag, inflow, ax_out, az_out, ra_out, outlet_out,
    pred, wide, diag, tell_a, hear_a, tell_b, hear_b, sums,
    send_a, recv_a, send_b, recv_b, send_s, recv_s,
):
    layers, rows, cells = ax.shape
    me = lax.axis_index("az")
    sleeve = lax.axis_index("sec") == 1
    right, left = lax.rem(me + 1, n), lax.rem(me + n - 1, n)
    fields = (ax, az, ra)
    outs = (ax_out, az_out, ra_out)

    barrier = pltpu.get_barrier_semaphore()

    def greet(k, carry):
        pl.semaphore_signal(barrier, inc=1, device_id={"az": lax.rem(me + k, n)}, device_id_type=MESH)
        return carry

    lax.fori_loop(1, n, greet, 0)

    lane = lax.broadcasted_iota(jnp.int32, (rows, cells), 1)
    flags = drag[...].astype(jnp.float32)
    spread = jnp.zeros((rows, cells), jnp.float32)
    for block in range(drag.shape[1]):
        spread = jnp.where(lane // block_cells == block, flags[:, block : block + 1], spread)
    diag[...] = jnp.zeros_like(diag)
    diag[0:rows, :] = 4.0 + diagonal_add - centre + drag_rate * spread

    for f in range(3):
        for l in range(layers):
            at = f * layers + l
            tell_a[0, at : at + 1, :] = fields[f][l, 0:1, :]
            tell_a[1, at : at + 1, :] = fields[f][l, rows - 1 : rows, :]
    at = 3 * layers
    tell_a[0, at : at + 2, :] = diag[0:2, :]
    tell_a[1, at : at + 1, :] = diag[rows - 1 : rows, :]
    pl.semaphore_wait(barrier, n - 1)

    def exchange(tell, hear, send, recv):
        copies = []
        for slot, to in ((0, left), (1, right)):
            copy = pltpu.make_async_remote_copy(
                src_ref=tell.at[slot], dst_ref=hear.at[slot],
                send_sem=send.at[slot], recv_sem=recv.at[slot],
                device_id={"az": to}, device_id_type=MESH,
            )
            copy.start()
            copies.append(copy)
        return copies

    copies_a = exchange(tell_a, hear_a, send_a, recv_a)
    for copy in copies_a:
        copy.wait()
    diag[rows : rows + 2, :] = hear_a[0, at : at + 2, :]
    diag[2 * rows - 1 : 2 * rows, :] = hear_a[1, at : at + 1, :]

    row = lax.broadcasted_iota(jnp.int32, (rows, cells), 0)
    for f in range(3):
        own_outlet = fields[f][layers - 1]
        turned = jnp.concatenate([inflow[f, pl.ds(pairs[j], 1), :] for j in range(rows)], axis=0)
        upstream = jnp.where(sleeve, turned, own_outlet)
        for l in range(layers):
            x = fields[f][l]
            above = jnp.where(row == 0, hear_a[1, f * layers + l : f * layers + l + 1, :], pltpu.roll(x, 1, 0))
            below = jnp.where(
                row == rows - 1, hear_a[0, f * layers + l : f * layers + l + 1, :], pltpu.roll(x, rows - 1, 0)
            )
            around = above + below + radial_sum(x)
            pred[f, l] = x - courant * (x - upstream) + viscosity * (around - 4.0 * x)
            upstream = x

    for l in range(layers):
        v, w = pred[1, l], pred[2, l]
        v_prev = jnp.where(row == 0, 0.0, pltpu.roll(v, 1, 0))
        w_prev = jnp.where(lane == 0, 0.0, pltpu.roll(w, 1, 1))
        wide[l, 0:rows, :] = v - v_prev + (w - w_prev)
        tell_b[0, 4 * l : 4 * l + 3, :] = wide[l, 0:3, :]
        tell_b[1, 4 * l : 4 * l + 2, :] = wide[l, rows - 2 : rows, :]
        tell_b[1, 4 * l + 2 : 4 * l + 3, :] = v[rows - 1 : rows, :]
    copies_b = exchange(tell_b, hear_b, send_b, recv_b)
    for copy in copies_b:
        copy.wait()

    c_diag = diag[...]

    def apply(x):
        ring = 2 * rows
        return c_diag * x - (pltpu.roll(x, 1, 0) + pltpu.roll(x, ring - 1, 0) + radial_sum(x))

    def total(x):
        folded = x[:, 0:128]
        for c in range(1, cells // 128):
            folded = folded + x[:, c * 128 : (c + 1) * 128]
        return jnp.sum(folded, axis=0, keepdims=True)

    basis = []
    for l in range(layers):
        wide[l, 0:1, :] = wide[l, 0:1, :] - hear_b[1, 4 * l + 2 : 4 * l + 3, :]
        wide[l, rows : 2 * rows, :] = jnp.zeros((rows, cells), jnp.float32)
        wide[l, rows : rows + 1, :] = hear_b[0, 4 * l : 4 * l + 1, :] - pred[1, l, rows - 1 : rows, :]
        wide[l, rows + 1 : rows + 3, :] = hear_b[0, 4 * l + 1 : 4 * l + 3, :]
        wide[l, 2 * rows - 2 : 2 * rows, :] = hear_b[1, 4 * l : 4 * l + 2, :]
        b = wide[l]
        v1 = apply(b)
        v2 = apply(v1)
        b0, b1, b2 = b[0:rows], v1[0:rows], v2[0:rows]
        next_row = pltpu.roll(v2, 2 * rows - 1, 0)[0:rows]
        next_cell = jnp.where(lane == cells - 1, 0.0, pltpu.roll(b2, cells - 1, 1))
        parts = (b0 * b0, b0 * b1, b1 * b1, b1 * b2, b2 * b2, b2 * (c_diag[0:rows] * b2 - 2.0 * (next_row + next_cell)))
        for k, part in enumerate(parts):
            sums[me, k, l : l + 1, :] = total(part)
        basis.append((v1, v2))

    def sum_copy(k, slot_of):
        return pltpu.make_async_remote_copy(
            src_ref=sums.at[me], dst_ref=sums.at[slot_of],
            send_sem=send_s.at[k], recv_sem=recv_s.at[slot_of],
            device_id={"az": lax.rem(me + k, n)}, device_id_type=MESH,
        )

    def give(k, carry):
        sum_copy(k, me).start()
        return carry

    def take(k, carry):
        sum_copy(k, me).wait_send()
        sum_copy(k, lax.rem(me + n - k, n)).wait_recv()
        return carry

    lax.fori_loop(1, n, give, 0)
    lax.fori_loop(1, n, take, 0)

    moments = lax.fori_loop(1, n, lambda j, acc: acc + sums[j], sums[0])
    m = [jnp.sum(moments[k], axis=1, keepdims=True) for k in range(6)]
    g = [m[k + 1] + centre * m[k] for k in range(5)]
    inv0 = 1.0 / g[0]
    l10, l20 = g[1] * inv0, g[2] * inv0
    d1 = g[2] - l10 * g[1]
    inv1 = jnp.where(d1 > 1e-7 * g[2], 1.0 / d1, 0.0)
    t21 = g[3] - l20 * g[1]
    l21 = t21 * inv1
    d2 = g[4] - l20 * g[2] - l21 * t21
    inv2 = jnp.where(d2 > 1e-7 * g[4], 1.0 / d2, 0.0)
    y0 = m[0]
    y1 = m[1] - l10 * y0
    y2 = m[2] - l20 * y0 - l21 * y1
    c2 = y2 * inv2
    c1 = y1 * inv1 - l21 * c2
    c0 = y0 * inv0 - l10 * c1 - l20 * c2

    for l in range(layers):
        v1, v2 = basis[l]
        pressure = c0[l : l + 1] * wide[l] + c1[l : l + 1] * v1 + c2[l : l + 1] * v2
        p = pressure[0:rows]
        p_row = pltpu.roll(pressure, 2 * rows - 1, 0)[0:rows]
        p_cell = jnp.where(lane == cells - 1, 0.0, pltpu.roll(p, cells - 1, 1))
        results = (pred[0, l], pred[1, l] - (p_row - p), pred[2, l] - (p_cell - p))
        for f in range(3):
            outs[f][l] = results[f]
            if l == layers - 1:
                outlet_out[f] = results[f]


def step(n, pairs, ax, az, ra, drag, inflow):
    layers, rows, cells = ax.shape
    f32 = jnp.float32
    vmem = pl.BlockSpec(memory_space=pltpu.VMEM)
    field = jax.ShapeDtypeStruct(ax.shape, f32)
    told = -(-(3 * layers + 2) // 8) * 8
    return pl.pallas_call(
        functools.partial(step_kernel, n),
        out_shape=(field, field, field, jax.ShapeDtypeStruct((3, rows, cells), f32)),
        in_specs=[pl.BlockSpec(memory_space=pltpu.SMEM)] + [vmem] * 5,
        out_specs=(vmem,) * 4,
        scratch_shapes=[
            pltpu.VMEM((3, layers, rows, cells), f32),
            pltpu.VMEM((layers, 2 * rows, cells), f32),
            pltpu.VMEM((2 * rows, cells), f32),
            pltpu.VMEM((2, told, cells), f32),
            pltpu.VMEM((2, told, cells), f32),
            pltpu.VMEM((2, 4 * layers, cells), f32),
            pltpu.VMEM((2, 4 * layers, cells), f32),
            pltpu.VMEM((n, 6, layers, 128), f32),
            pltpu.SemaphoreType.DMA((2,)),
            pltpu.SemaphoreType.DMA((2,)),
            pltpu.SemaphoreType.DMA((2,)),
            pltpu.SemaphoreType.DMA((2,)),
            pltpu.SemaphoreType.DMA((n,)),
            pltpu.SemaphoreType.DMA((n,)),
        ],
        compiler_params=pltpu.CompilerParams(
            collective_id=0, has_side_effects=True, vmem_limit_bytes=24 * 1024 * 1024
        ),
    )(pairs, ax, az, ra, drag, inflow)


def turned_inflow(outlet, turn, n):
    def route(shift):
        pairs = [(b, n + (b + shift) % n) for b in range(n)]
        return lambda plane: lax.ppermute(plane, ("sec", "az"), pairs)

    return lax.switch(turn, [route(shift) for shift in range(n)], outlet)


def body(axial, azimuthal, radial, drag_blocks, rotation, row_pairs):
    n = lax.axis_size("az")
    ax, az, ra, drag = axial[0], azimuthal[0], radial[0], drag_blocks[0]
    outlet = jnp.stack([ax[-1], az[-1], ra[-1]])
    for time_step in range(STEPS):
        inflow = turned_inflow(outlet, rotation[0] * (time_step + 1) % n, n)
        ax, az, ra, outlet = step(n, row_pairs, ax, az, ra, drag, inflow)
    return ax[None], az[None], ra[None]


def solution(mesh):
    field = P("sec", None, "az", None)
    return jax.shard_map(
        body,
        mesh=mesh,
        in_specs=(field, field, field, P("sec", "az", None), P(), P()),
        out_specs=(field, field, field),
        check_vma=False,
    )
```

```python
import functools

import jax
import jax.numpy as jnp
from jax import lax
from jax.experimental import pallas as pl
from jax.experimental.pallas import tpu as pltpu
from jax.sharding import PartitionSpec as P

STEPS = 2

courant = 0.5
viscosity = 0.1
diagonal_add = 0.05
drag_rate = 2.0
block_cells = 64
centre = 4.0 + diagonal_add + 0.5 * drag_rate
MESH = pl.DeviceIdType.MESH


def radial_sum(x):
    cells = x.shape[1]
    lane = lax.broadcasted_iota(jnp.int32, x.shape, 1)
    before = jnp.where(lane == 0, 0.0, pltpu.roll(x, 1, 1))
    after = jnp.where(lane == cells - 1, 0.0, pltpu.roll(x, cells - 1, 1))
    return before + after


def steps_kernel(
    n, pairs, rotation, ax, az, ra, drag, ax_out, az_out, ra_out,
    mid, pred, wide, diag, tell_a, hear_a, tell_b, hear_b, sums, plane, got, inflow, landing,
    send_a, recv_a, send_b, recv_b, send_s, recv_s, send_p, recv_p, send_x, recv_x,
):
    layers, rows, cells = ax.shape
    stages = got.shape[0]
    me = lax.axis_index("az")
    sleeve = lax.axis_index("sec") == 1
    precursor = lax.axis_index("sec") == 0
    right, left = lax.rem(me + 1, n), lax.rem(me + n - 1, n)

    barrier = pltpu.get_barrier_semaphore()

    def greet(k, carry):
        pl.semaphore_signal(barrier, inc=1, device_id={"az": lax.rem(me + k, n)}, device_id_type=MESH)
        return carry

    lax.fori_loop(1, n, greet, 0)
    pl.semaphore_signal(
        barrier, inc=1, device_id={"sec": 1 - lax.axis_index("sec")}, device_id_type=MESH
    )

    lane = lax.broadcasted_iota(jnp.int32, (rows, cells), 1)
    row = lax.broadcasted_iota(jnp.int32, (rows, cells), 0)
    flags = drag[...].astype(jnp.float32)
    spread = jnp.zeros((rows, cells), jnp.float32)
    for block in range(drag.shape[1]):
        spread = jnp.where(lane // block_cells == block, flags[:, block : block + 1], spread)
    diag[...] = jnp.zeros_like(diag)
    diag[0:rows, :] = 4.0 + diagonal_add - centre + drag_rate * spread

    def exchange(tell, hear, send, recv):
        copies = []
        for slot, to in ((0, left), (1, right)):
            copy = pltpu.make_async_remote_copy(
                src_ref=tell.at[slot], dst_ref=hear.at[slot],
                send_sem=send.at[slot], recv_sem=recv.at[slot],
                device_id={"az": to}, device_id_type=MESH,
            )
            copy.start()
            copies.append(copy)
        return copies

    def cross(which, f, src, dst):
        return pltpu.make_async_remote_copy(
            src_ref=src, dst_ref=dst, send_sem=send_x.at[which, f], recv_sem=recv_x.at[which, f],
            device_id={"sec": 1}, device_id_type=MESH,
        )

    def stage_copy(k, f):
        return pltpu.make_async_remote_copy(
            src_ref=plane.at[k, f], dst_ref=got.at[k, f],
            send_sem=send_p.at[k, f], recv_sem=recv_p.at[k, f],
            device_id={"az": lax.rem(me + (1 << k) % n, n)}, device_id_type=MESH,
        )

    def turn_plane(turn, ready=None):
        for f in range(3):
            if ready is not None:
                ready(f)
            stage_copy(0, f).start()
        for k in range(stages):
            moves = lax.rem(lax.div(turn, 1 << k), 2) == 1
            for f in range(3):
                stage_copy(k, f).wait_recv()
                plane[k + 1, f] = jnp.where(moves, got[k, f], plane[k, f])
                if k + 1 < stages:
                    stage_copy(k + 1, f).start()

    def turn_sent():
        for k in range(stages):
            for f in range(3):
                stage_copy(k, f).wait_send()

    c_rows = 3 * layers
    for time_step in range(STEPS):
        first, last = time_step == 0, time_step == STEPS - 1
        fields = (ax, az, ra) if first else tuple(mid.at[f] for f in range(3))
        outs = (ax_out, az_out, ra_out) if last else tuple(mid.at[f] for f in range(3))
        turn = lax.rem(rotation[0] * (time_step + 1), n)
        ta, ha = tell_a.at[time_step], hear_a.at[time_step]
        tb, hb = tell_b.at[time_step], hear_b.at[time_step]
        ss = sums.at[time_step]

        for f in range(3):
            for l in range(layers):
                at = f * layers + l
                ta[0, at : at + 1, :] = fields[f][l, 0:1, :]
                ta[1, at : at + 1, :] = fields[f][l, rows - 1 : rows, :]
        if first:
            ta[0, c_rows : c_rows + 2, :] = diag[0:2, :]
            ta[1, c_rows : c_rows + 1, :] = diag[rows - 1 : rows, :]
            pl.semaphore_wait(barrier, n)

            @pl.when(precursor)
            def _():
                for f in range(3):
                    cross(0, f, (ax, az, ra)[f].at[layers - 1], plane.at[0, f]).start()

        copies_a = exchange(ta, ha, send_a.at[time_step], recv_a.at[time_step])
        if first:
            @pl.when(sleeve)
            def _():
                turn_plane(turn, lambda f: cross(0, f, plane.at[0, f], plane.at[0, f]).wait_recv())
        else:
            @pl.when(precursor)
            def _():
                for f in range(3):
                    plane[0, f] = fields[f][layers - 1]
                turn_plane(turn)
                for f in range(3):
                    cross(1, f, plane.at[stages, f], landing.at[f]).start()
                turn_sent()

        for copy in copies_a:
            copy.wait()
        if first:
            diag[rows : rows + 2, :] = ha[0, c_rows : c_rows + 2, :]
            diag[2 * rows - 1 : 2 * rows, :] = ha[1, c_rows : c_rows + 1, :]

            @pl.when(sleeve)
            def _():
                for f in range(3):
                    inflow[f] = plane[stages, f]
                turn_sent()

            @pl.when(precursor)
            def _():
                for f in range(3):
                    cross(0, f, (ax, az, ra)[f].at[layers - 1], plane.at[0, f]).wait_send()
                    inflow[f] = (ax, az, ra)[f][layers - 1]
        else:
            @pl.when(sleeve)
            def _():
                for f in range(3):
                    cross(1, f, plane.at[stages, f], landing.at[f]).wait_recv()
                    inflow[f] = landing[f]

        for f in range(3):
            turned = jnp.concatenate([inflow[f, pl.ds(pairs[j], 1), :] for j in range(rows)], axis=0)
            upstream = jnp.where(sleeve, turned, fields[f][layers - 1])
            for l in range(layers):
                x = fields[f][l]
                at = f * layers + l
                above = jnp.where(row == 0, ha[1, at : at + 1, :], pltpu.roll(x, 1, 0))
                below = jnp.where(row == rows - 1, ha[0, at : at + 1, :], pltpu.roll(x, rows - 1, 0))
                around = above + below + radial_sum(x)
                pred[f, l] = x - courant * (x - upstream) + viscosity * (around - 4.0 * x)
                upstream = x

        for l in range(layers):
            v, w = pred[1, l], pred[2, l]
            v_prev = jnp.where(row == 0, 0.0, pltpu.roll(v, 1, 0))
            w_prev = jnp.where(lane == 0, 0.0, pltpu.roll(w, 1, 1))
            wide[l, 0:rows, :] = v - v_prev + (w - w_prev)
            tb[0, 4 * l : 4 * l + 3, :] = wide[l, 0:3, :]
            tb[1, 4 * l : 4 * l + 2, :] = wide[l, rows - 2 : rows, :]
            tb[1, 4 * l + 2 : 4 * l + 3, :] = v[rows - 1 : rows, :]
        for copy in exchange(tb, hb, send_b.at[time_step], recv_b.at[time_step]):
            copy.wait()

        c_diag = diag[...]

        def apply(x):
            ring = 2 * rows
            return c_diag * x - (pltpu.roll(x, 1, 0) + pltpu.roll(x, ring - 1, 0) + radial_sum(x))

        def total(x):
            folded = x[:, 0:128]
            for c in range(1, cells // 128):
                folded = folded + x[:, c * 128 : (c + 1) * 128]
            return jnp.sum(folded, axis=0, keepdims=True)

        basis = []
        for l in range(layers):
            wide[l, 0:1, :] = wide[l, 0:1, :] - hb[1, 4 * l + 2 : 4 * l + 3, :]
            wide[l, rows : 2 * rows, :] = jnp.zeros((rows, cells), jnp.float32)
            wide[l, rows : rows + 1, :] = hb[0, 4 * l : 4 * l + 1, :] - pred[1, l, rows - 1 : rows, :]
            wide[l, rows + 1 : rows + 3, :] = hb[0, 4 * l + 1 : 4 * l + 3, :]
            wide[l, 2 * rows - 2 : 2 * rows, :] = hb[1, 4 * l : 4 * l + 2, :]
            b = wide[l]
            v1 = apply(b)
            v2 = apply(v1)
            b0, b1, b2 = b[0:rows], v1[0:rows], v2[0:rows]
            next_row = pltpu.roll(v2, 2 * rows - 1, 0)[0:rows]
            next_cell = jnp.where(lane == cells - 1, 0.0, pltpu.roll(b2, cells - 1, 1))
            c_b2 = c_diag[0:rows] * b2 - 2.0 * (next_row + next_cell)
            parts = (b0 * b0, b0 * b1, b1 * b1, b1 * b2, b2 * b2, b2 * c_b2)
            for k, part in enumerate(parts):
                ss[me, k, l : l + 1, :] = total(part)
            basis.append((v1, v2))

        def sum_copy(k, slot_of):
            return pltpu.make_async_remote_copy(
                src_ref=ss.at[me], dst_ref=ss.at[slot_of],
                send_sem=send_s.at[time_step, k], recv_sem=recv_s.at[time_step, slot_of],
                device_id={"az": lax.rem(me + k, n)}, device_id_type=MESH,
            )

        def give(k, carry):
            sum_copy(k, me).start()
            return carry

        def take(k, carry):
            sum_copy(k, me).wait_send()
            sum_copy(k, lax.rem(me + n - k, n)).wait_recv()
            return carry

        lax.fori_loop(1, n, give, 0)
        lax.fori_loop(1, n, take, 0)

        moments = lax.fori_loop(1, n, lambda j, acc: acc + ss[j], ss[0])
        m = [jnp.sum(moments[k], axis=1, keepdims=True) for k in range(6)]
        g = [m[k + 1] + centre * m[k] for k in range(5)]
        inv0 = 1.0 / g[0]
        l10, l20 = g[1] * inv0, g[2] * inv0
        d1 = g[2] - l10 * g[1]
        inv1 = jnp.where(d1 > 1e-7 * g[2], 1.0 / d1, 0.0)
        t21 = g[3] - l20 * g[1]
        l21 = t21 * inv1
        d2 = g[4] - l20 * g[2] - l21 * t21
        inv2 = jnp.where(d2 > 1e-7 * g[4], 1.0 / d2, 0.0)
        y0 = m[0]
        y1 = m[1] - l10 * y0
        y2 = m[2] - l20 * y0 - l21 * y1
        c2 = y2 * inv2
        c1 = y1 * inv1 - l21 * c2
        c0 = y0 * inv0 - l10 * c1 - l20 * c2

        for l in range(layers):
            v1, v2 = basis[l]
            pressure = c0[l : l + 1] * wide[l] + c1[l : l + 1] * v1 + c2[l : l + 1] * v2
            p = pressure[0:rows]
            p_row = pltpu.roll(pressure, 2 * rows - 1, 0)[0:rows]
            p_cell = jnp.where(lane == cells - 1, 0.0, pltpu.roll(p, cells - 1, 1))
            outs[0][l] = pred[0, l]
            outs[1][l] = pred[1, l] - (p_row - p)
            outs[2][l] = pred[2, l] - (p_cell - p)

    @pl.when(precursor)
    def _():
        for f in range(3):
            cross(1, f, plane.at[stages, f], landing.at[f]).wait_send()


def steps(n, pairs, rotation, ax, az, ra, drag):
    layers, rows, cells = ax.shape
    f32 = jnp.float32
    stages = (n - 1).bit_length()
    vmem, smem = pl.BlockSpec(memory_space=pltpu.VMEM), pl.BlockSpec(memory_space=pltpu.SMEM)
    field = jax.ShapeDtypeStruct(ax.shape, f32)
    told = -(-(3 * layers + 2) // 8) * 8
    dma = pltpu.SemaphoreType.DMA
    return pl.pallas_call(
        functools.partial(steps_kernel, n),
        out_shape=(field, field, field),
        in_specs=[smem, smem] + [vmem] * 4,
        out_specs=(vmem,) * 3,
        scratch_shapes=[
            pltpu.VMEM((3, layers, rows, cells), f32),
            pltpu.VMEM((3, layers, rows, cells), f32),
            pltpu.VMEM((layers, 2 * rows, cells), f32),
            pltpu.VMEM((2 * rows, cells), f32),
            pltpu.VMEM((STEPS, 2, told, cells), f32),
            pltpu.VMEM((STEPS, 2, told, cells), f32),
            pltpu.VMEM((STEPS, 2, 4 * layers, cells), f32),
            pltpu.VMEM((STEPS, 2, 4 * layers, cells), f32),
            pltpu.VMEM((STEPS, n, 6, layers, 128), f32),
            pltpu.VMEM((stages + 1, 3, rows, cells), f32),
            pltpu.VMEM((stages, 3, rows, cells), f32),
            pltpu.VMEM((3, rows, cells), f32),
            pltpu.VMEM((3, rows, cells), f32),
            dma((STEPS, 2)),
            dma((STEPS, 2)),
            dma((STEPS, 2)),
            dma((STEPS, 2)),
            dma((STEPS, n)),
            dma((STEPS, n)),
            dma((stages, 3)),
            dma((stages, 3)),
            dma((2, 3)),
            dma((2, 3)),
        ],
        compiler_params=pltpu.CompilerParams(
            collective_id=0, has_side_effects=True, vmem_limit_bytes=32 * 1024 * 1024
        ),
    )(pairs, rotation, ax, az, ra, drag)


def body(axial, azimuthal, radial, drag_blocks, rotation, row_pairs):
    n = lax.axis_size("az")
    outs = steps(n, row_pairs, rotation, axial[0], azimuthal[0], radial[0], drag_blocks[0])
    return tuple(out[None] for out in outs)


def solution(mesh):
    field = P("sec", None, "az", None)
    return jax.shard_map(
        body,
        mesh=mesh,
        in_specs=(field, field, field, P("sec", "az", None), P(), P()),
        out_specs=(field, field, field),
        check_vma=False,
    )
```

```python
import functools

import jax
import jax.numpy as jnp
from jax import lax
from jax.experimental import pallas as pl
from jax.experimental.pallas import tpu as pltpu
from jax.sharding import PartitionSpec as P

STEPS = 2

courant = 0.5
viscosity = 0.1
diagonal_add = 0.05
drag_rate = 2.0
block_cells = 64
centre = 4.0 + diagonal_add + 0.5 * drag_rate
MESH = pl.DeviceIdType.MESH


def radial_sum(x):
    cells = x.shape[1]
    lane = lax.broadcasted_iota(jnp.int32, x.shape, 1)
    before = jnp.where(lane == 0, 0.0, pltpu.roll(x, 1, 1))
    after = jnp.where(lane == cells - 1, 0.0, pltpu.roll(x, cells - 1, 1))
    return before + after


def steps_kernel(
    n, pairs, rotation, ax_in, az_in, ra_in, drag, ax_out, az_out, ra_out,
    held, mid, pred, wide, diag, tell_a, hear_a, tell_b, hear_b, folds, sums, plane, got, inflow, landing,
    send_a, recv_a, send_b, recv_b, send_s, recv_s, send_p, recv_p, send_x, recv_x, load_sem,
):
    layers, rows, cells = ax_in.shape
    ax, az, ra = (held.at[f] for f in range(3))
    loads = [pltpu.make_async_copy(src, held.at[f], load_sem.at[f]) for f, src in enumerate((ax_in, az_in, ra_in))]
    for load in loads:
        load.start()
    stages = got.shape[0]
    me = lax.axis_index("az")
    sleeve = lax.axis_index("sec") == 1
    precursor = lax.axis_index("sec") == 0
    right, left = lax.rem(me + 1, n), lax.rem(me + n - 1, n)

    barrier = pltpu.get_barrier_semaphore()

    def greet(k, carry):
        pl.semaphore_signal(barrier, inc=1, device_id={"az": lax.rem(me + k, n)}, device_id_type=MESH)
        return carry

    lax.fori_loop(1, n, greet, 0)
    pl.semaphore_signal(
        barrier, inc=1, device_id={"sec": 1 - lax.axis_index("sec")}, device_id_type=MESH
    )

    lane = lax.broadcasted_iota(jnp.int32, (rows, cells), 1)
    row = lax.broadcasted_iota(jnp.int32, (rows, cells), 0)
    flags = drag[...].astype(jnp.float32)
    spread = jnp.zeros((rows, cells), jnp.float32)
    for block in range(drag.shape[1]):
        spread = jnp.where(lane // block_cells == block, flags[:, block : block + 1], spread)
    diag[...] = jnp.zeros_like(diag)
    diag[0:rows, :] = 4.0 + diagonal_add - centre + drag_rate * spread

    for load in loads:
        load.wait()

    def exchange(tell, hear, send, recv):
        copies = []
        for slot, to in ((0, left), (1, right)):
            copy = pltpu.make_async_remote_copy(
                src_ref=tell.at[slot], dst_ref=hear.at[slot],
                send_sem=send.at[slot], recv_sem=recv.at[slot],
                device_id={"az": to}, device_id_type=MESH,
            )
            copy.start()
            copies.append(copy)
        return copies

    def cross(which, f, src, dst):
        return pltpu.make_async_remote_copy(
            src_ref=src, dst_ref=dst, send_sem=send_x.at[which, f], recv_sem=recv_x.at[which, f],
            device_id={"sec": 1}, device_id_type=MESH,
        )

    def stage_copy(k, f):
        return pltpu.make_async_remote_copy(
            src_ref=plane.at[k, f], dst_ref=got.at[k, f],
            send_sem=send_p.at[k, f], recv_sem=recv_p.at[k, f],
            device_id={"az": lax.rem(me + (1 << k) % n, n)}, device_id_type=MESH,
        )

    def turn_plane(turn, ready=None):
        for f in range(3):
            if ready is not None:
                ready(f)
            stage_copy(0, f).start()
        for k in range(stages):
            moves = lax.rem(lax.div(turn, 1 << k), 2) == 1
            for f in range(3):
                stage_copy(k, f).wait_recv()
                plane[k + 1, f] = jnp.where(moves, got[k, f], plane[k, f])
                if k + 1 < stages:
                    stage_copy(k + 1, f).start()

    def turn_sent():
        for k in range(stages):
            for f in range(3):
                stage_copy(k, f).wait_send()

    c_rows = 3 * layers
    for time_step in range(STEPS):
        first, last = time_step == 0, time_step == STEPS - 1
        fields = (ax, az, ra) if first else tuple(mid.at[f] for f in range(3))
        outs = (ax_out, az_out, ra_out) if last else tuple(mid.at[f] for f in range(3))
        turn = lax.rem(rotation[0] * (time_step + 1), n)
        ta, ha = tell_a.at[time_step], hear_a.at[time_step]
        tb, hb = tell_b.at[time_step], hear_b.at[time_step]
        ss = sums.at[time_step]

        for f in range(3):
            for l in range(layers):
                at = f * layers + l
                ta[0, at : at + 1, :] = fields[f][l, 0:1, :]
                ta[1, at : at + 1, :] = fields[f][l, rows - 1 : rows, :]
        if first:
            ta[0, c_rows : c_rows + 2, :] = diag[0:2, :]
            ta[1, c_rows : c_rows + 1, :] = diag[rows - 1 : rows, :]
            pl.semaphore_wait(barrier, n)

            @pl.when(precursor)
            def _():
                for f in range(3):
                    cross(0, f, (ax, az, ra)[f].at[layers - 1], plane.at[0, f]).start()

        copies_a = exchange(ta, ha, send_a.at[time_step], recv_a.at[time_step])
        if first:
            @pl.when(sleeve)
            def _():
                turn_plane(turn, lambda f: cross(0, f, plane.at[0, f], plane.at[0, f]).wait_recv())
        else:
            @pl.when(precursor)
            def _():
                for f in range(3):
                    plane[0, f] = fields[f][layers - 1]
                turn_plane(turn)
                for f in range(3):
                    cross(1, f, plane.at[stages, f], landing.at[f]).start()
                turn_sent()

        for copy in copies_a:
            copy.wait()
        if first:
            diag[rows : rows + 2, :] = ha[0, c_rows : c_rows + 2, :]
            diag[2 * rows - 1 : 2 * rows, :] = ha[1, c_rows : c_rows + 1, :]

            @pl.when(sleeve)
            def _():
                for f in range(3):
                    inflow[f] = plane[stages, f]
                turn_sent()

            @pl.when(precursor)
            def _():
                for f in range(3):
                    cross(0, f, (ax, az, ra)[f].at[layers - 1], plane.at[0, f]).wait_send()
                    inflow[f] = (ax, az, ra)[f][layers - 1]
        else:
            @pl.when(sleeve)
            def _():
                for f in range(3):
                    cross(1, f, plane.at[stages, f], landing.at[f]).wait_recv()
                    inflow[f] = landing[f]

        for f in range(3):
            turned = jnp.concatenate([inflow[f, pl.ds(pairs[j], 1), :] for j in range(rows)], axis=0)
            upstream = jnp.where(sleeve, turned, fields[f][layers - 1])
            for l in range(layers):
                x = fields[f][l]
                at = f * layers + l
                above = jnp.where(row == 0, ha[1, at : at + 1, :], pltpu.roll(x, 1, 0))
                below = jnp.where(row == rows - 1, ha[0, at : at + 1, :], pltpu.roll(x, rows - 1, 0))
                around = above + below + radial_sum(x)
                pred[f, l] = x - courant * (x - upstream) + viscosity * (around - 4.0 * x)
                upstream = x

        for l in range(layers):
            v, w = pred[1, l], pred[2, l]
            v_prev = jnp.where(row == 0, 0.0, pltpu.roll(v, 1, 0))
            w_prev = jnp.where(lane == 0, 0.0, pltpu.roll(w, 1, 1))
            wide[l, 0:rows, :] = v - v_prev + (w - w_prev)
            tb[0, 4 * l : 4 * l + 3, :] = wide[l, 0:3, :]
            tb[1, 4 * l : 4 * l + 2, :] = wide[l, rows - 2 : rows, :]
            tb[1, 4 * l + 2 : 4 * l + 3, :] = v[rows - 1 : rows, :]
        for copy in exchange(tb, hb, send_b.at[time_step], recv_b.at[time_step]):
            copy.wait()

        c_diag = diag[...]

        def apply(x):
            ring = 2 * rows
            return c_diag * x - (pltpu.roll(x, 1, 0) + pltpu.roll(x, ring - 1, 0) + radial_sum(x))

        def total(x):
            folded = x[:, 0:128]
            for c in range(1, cells // 128):
                folded = folded + x[:, c * 128 : (c + 1) * 128]
            return jnp.sum(folded, axis=0, keepdims=True)

        basis = []
        for l in range(layers):
            wide[l, 0:1, :] = wide[l, 0:1, :] - hb[1, 4 * l + 2 : 4 * l + 3, :]
            wide[l, rows : 2 * rows, :] = jnp.zeros((rows, cells), jnp.float32)
            wide[l, rows : rows + 1, :] = hb[0, 4 * l : 4 * l + 1, :] - pred[1, l, rows - 1 : rows, :]
            wide[l, rows + 1 : rows + 3, :] = hb[0, 4 * l + 1 : 4 * l + 3, :]
            wide[l, 2 * rows - 2 : 2 * rows, :] = hb[1, 4 * l : 4 * l + 2, :]
            b = wide[l]
            v1 = apply(b)
            v2 = apply(v1)
            b0, b1, b2 = b[0:rows], v1[0:rows], v2[0:rows]
            next_row = pltpu.roll(v2, 2 * rows - 1, 0)[0:rows]
            next_cell = jnp.where(lane == cells - 1, 0.0, pltpu.roll(b2, cells - 1, 1))
            c_b2 = c_diag[0:rows] * b2 - 2.0 * (next_row + next_cell)
            parts = (b0 * b0, b0 * b1, b1 * b1, b1 * b2, b2 * b2, b2 * c_b2)
            for k, part in enumerate(parts):
                folds[k, l : l + 1, :] = total(part)
            basis.append((v1, v2))

        slot = lax.broadcasted_iota(jnp.int32, (layers, 128), 1)
        packed = jnp.zeros((layers, 128), jnp.float32)
        for k in range(6):
            packed = jnp.where(slot == k, jnp.sum(folds[k], axis=1, keepdims=True), packed)
        ss[me] = packed

        def sum_copy(k, slot_of):
            return pltpu.make_async_remote_copy(
                src_ref=ss.at[me], dst_ref=ss.at[slot_of],
                send_sem=send_s.at[time_step, k], recv_sem=recv_s.at[time_step, slot_of],
                device_id={"az": lax.rem(me + k, n)}, device_id_type=MESH,
            )

        def give(k, carry):
            sum_copy(k, me).start()
            return carry

        def take(k, carry):
            sum_copy(k, me).wait_send()
            sum_copy(k, lax.rem(me + n - k, n)).wait_recv()
            return carry

        lax.fori_loop(1, n, give, 0)
        lax.fori_loop(1, n, take, 0)

        moments = lax.fori_loop(1, n, lambda j, acc: acc + ss[j], ss[0])
        m = [moments[:, k : k + 1] for k in range(6)]
        g = [m[k + 1] + centre * m[k] for k in range(5)]
        inv0 = 1.0 / g[0]
        l10, l20 = g[1] * inv0, g[2] * inv0
        d1 = g[2] - l10 * g[1]
        inv1 = jnp.where(d1 > 1e-7 * g[2], 1.0 / d1, 0.0)
        t21 = g[3] - l20 * g[1]
        l21 = t21 * inv1
        d2 = g[4] - l20 * g[2] - l21 * t21
        inv2 = jnp.where(d2 > 1e-7 * g[4], 1.0 / d2, 0.0)
        y0 = m[0]
        y1 = m[1] - l10 * y0
        y2 = m[2] - l20 * y0 - l21 * y1
        c2 = y2 * inv2
        c1 = y1 * inv1 - l21 * c2
        c0 = y0 * inv0 - l10 * c1 - l20 * c2

        for l in range(layers):
            v1, v2 = basis[l]
            pressure = c0[l : l + 1] * wide[l] + c1[l : l + 1] * v1 + c2[l : l + 1] * v2
            p = pressure[0:rows]
            p_row = pltpu.roll(pressure, 2 * rows - 1, 0)[0:rows]
            p_cell = jnp.where(lane == cells - 1, 0.0, pltpu.roll(p, cells - 1, 1))
            outs[0][l] = pred[0, l]
            outs[1][l] = pred[1, l] - (p_row - p)
            outs[2][l] = pred[2, l] - (p_cell - p)

    @pl.when(precursor)
    def _():
        for f in range(3):
            cross(1, f, plane.at[stages, f], landing.at[f]).wait_send()


def steps(n, pairs, rotation, ax, az, ra, drag):
    layers, rows, cells = ax.shape
    f32 = jnp.float32
    stages = (n - 1).bit_length()
    vmem, smem = pl.BlockSpec(memory_space=pltpu.VMEM), pl.BlockSpec(memory_space=pltpu.SMEM)
    field = jax.ShapeDtypeStruct(ax.shape, f32)
    told = -(-(3 * layers + 2) // 8) * 8
    dma = pltpu.SemaphoreType.DMA
    return pl.pallas_call(
        functools.partial(steps_kernel, n),
        out_shape=(field, field, field),
        in_specs=[smem, smem] + [pl.BlockSpec(memory_space=pltpu.HBM)] * 3 + [vmem],
        out_specs=(vmem,) * 3,
        scratch_shapes=[
            pltpu.VMEM((3, layers, rows, cells), f32),
            pltpu.VMEM((3, layers, rows, cells), f32),
            pltpu.VMEM((3, layers, rows, cells), f32),
            pltpu.VMEM((layers, 2 * rows, cells), f32),
            pltpu.VMEM((2 * rows, cells), f32),
            pltpu.VMEM((STEPS, 2, told, cells), f32),
            pltpu.VMEM((STEPS, 2, told, cells), f32),
            pltpu.VMEM((STEPS, 2, 4 * layers, cells), f32),
            pltpu.VMEM((STEPS, 2, 4 * layers, cells), f32),
            pltpu.VMEM((6, layers, 128), f32),
            pltpu.VMEM((STEPS, n, layers, 128), f32),
            pltpu.VMEM((stages + 1, 3, rows, cells), f32),
            pltpu.VMEM((stages, 3, rows, cells), f32),
            pltpu.VMEM((3, rows, cells), f32),
            pltpu.VMEM((3, rows, cells), f32),
            dma((STEPS, 2)),
            dma((STEPS, 2)),
            dma((STEPS, 2)),
            dma((STEPS, 2)),
            dma((STEPS, n)),
            dma((STEPS, n)),
            dma((stages, 3)),
            dma((stages, 3)),
            dma((2, 3)),
            dma((2, 3)),
            dma((3,)),
        ],
        compiler_params=pltpu.CompilerParams(
            collective_id=0, has_side_effects=True, vmem_limit_bytes=60 * 1024 * 1024
        ),
    )(pairs, rotation, ax, az, ra, drag)


def body(axial, azimuthal, radial, drag_blocks, rotation, row_pairs):
    n = lax.axis_size("az")
    outs = steps(n, row_pairs, rotation, axial[0], azimuthal[0], radial[0], drag_blocks[0])
    return tuple(out[None] for out in outs)


def solution(mesh):
    field = P("sec", None, "az", None)
    return jax.shard_map(
        body,
        mesh=mesh,
        in_specs=(field, field, field, P("sec", "az", None), P(), P()),
        out_specs=(field, field, field),
        check_vma=False,
    )
```
